256 devices in a mesh: row: 8 (over z), col: 16 (over x, y_lo, core), rep: 2 (over y_hi).
Axes of the slice: x: 4, y: 4 (y_hi: 2, y_lo: 2; y = y_hi * 2 + y_lo), z: 8, core: 2. Of those that a mesh axis runs over, the one named last changes fastest.
Arguments:
- a_blocks: bfloat16 [16384, 4096], P('row', 'col'), may hold values from -6 to 6
- a_mask: int32 [64, 16], P('row', 'col'), may hold values from 0 to 1, as said below
- b_blocks: bfloat16 [4096, 8192], P('row', 'col'), may hold values from -0.09375 to 0.09375
- b_mask: int32 [16, 32], P('row', 'col'), may hold values from 0 to 1
Outputs:
- c_product: bfloat16 [16384, 8192], P('row', ('col', 'rep'))
The draws below stay inside these ranges and needn't reach their ends.
Inputs may be any that keep to these rules, and one draw needn't show every extreme that they name: a_mask holds 0 or 1; within each aligned tile of 8 block rows by 1 inner blocks (one device's tile) at most 2 entries are 1, and some tile holds exactly 2.
All inputs are finite; a program needn't handle non-finite values.
Results may differ from the reference program's by a relative error of at most 0.007.
Values may be sent and summed in bfloat16 or wider, within the bound.
A program may use at most 64 MiB of HBM per device.

```python
import jax
import jax.numpy as jnp

BS = 256
MB = 8
KA = 1
AMOST = 2
MT = 64
KT = 16
NT = 32


def draw_a_mask(key, part):
    tile_rows = MT // MB
    tile_cols = KT // KA
    tile_cells = MB * KA
    key_patch, key_sparse, key_order = jax.random.split(jax.random.fold_in(key, 11), 3)
    row_place = jnp.arange(tile_rows, dtype=jnp.int32)[:, None]
    col_place = jnp.arange(tile_cols, dtype=jnp.int32)[None, :]
    centre = row_place * tile_cols // tile_rows
    distance = jnp.abs(col_place - centre)
    distance = jnp.minimum(distance, tile_cols - distance)
    patches = jax.random.randint(key_patch, (tile_rows, tile_cols), 0, 8) == 0
    sparse_count = jax.random.randint(key_sparse, (tile_rows, tile_cols), 0, AMOST // 2 + 1)
    counts = jnp.where((distance <= 1) | patches, AMOST, sparse_count)
    scores = jax.random.randint(key_order, (tile_rows, tile_cols, tile_cells), 0, 1 << 20) * tile_cells + jnp.arange(tile_cells, dtype=jnp.int32)
    ranking = jnp.argsort(jnp.argsort(scores, axis=-1), axis=-1)
    pattern = (ranking < counts[:, :, None]).astype(jnp.int32)
    pattern = pattern.reshape(tile_rows, tile_cols, MB, KA).transpose(0, 2, 1, 3)
    return pattern.reshape(MT, KT)


def draw_b_mask(key, part):
    inner_place = jnp.arange(KT, dtype=jnp.int32)[:, None]
    column_place = jnp.arange(NT, dtype=jnp.int32)[None, :]
    centre = inner_place * NT // KT
    distance = jnp.abs(column_place - centre)
    distance = jnp.minimum(distance, NT - distance)
    drawn = jax.random.randint(jax.random.fold_in(key, 23), (KT, NT), 0, 20)
    pattern = jnp.where(distance * 8 <= NT, drawn < 16, drawn < 3)
    return pattern.astype(jnp.int32)


def steps_of(rng, shape, shards, least, high):
    loudness, own = 1.0, jax.random.fold_in(rng, 6)
    for axis_at, blocks in shards:
        heights = jnp.exp(jax.random.uniform(jax.random.fold_in(own, axis_at), (blocks,), jnp.float32, least / len(shards), high / len(shards)))
        loudness = loudness * jnp.repeat(heights, shape[axis_at] // blocks).reshape([-1 if axis == axis_at else 1 for axis in range(len(shape))])
    return loudness


def bell_draw(key, dims, spread, reach, shards=(), kind=jnp.bfloat16):
    entries = spread * jax.random.normal(key, dims, jnp.float32)
    if shards:
        entries = entries * steps_of(key, dims, shards, -0.22, 0.18)
    return jnp.clip(entries, -reach, reach).astype(kind)


def setup_inputs(seed: int = 0) -> dict:
    arg_keys = jax.random.split(jax.random.key(seed), 5)
    return {
        "a_blocks": bell_draw(arg_keys[0], (MT * BS, KT * BS), 1.0, 6.0, ((0, 8), (1, 16))),
        "a_mask": draw_a_mask(jax.random.fold_in(arg_keys[4], 71), 0),
        "b_blocks": bell_draw(arg_keys[2], (KT * BS, NT * BS), (KT * BS) ** -0.5, 0.09375, ((0, 8), (1, 16))),
        "b_mask": draw_b_mask(jax.random.fold_in(arg_keys[4], 71), 0),
    }


def expand(values, pattern):
    block_rows = pattern.shape[0]
    block_cols = pattern.shape[1]
    shaped = values.reshape(block_rows, BS, block_cols, BS) * pattern[:, None, :, None].astype(jnp.bfloat16)
    return shaped.reshape(block_rows * BS, block_cols * BS)


def reference(a_blocks, a_mask, b_blocks, b_mask):
    masked_a = expand(a_blocks, a_mask)
    masked_b = expand(b_blocks, b_mask)
    return jnp.dot(masked_a, masked_b, preferred_element_type=jnp.float32).astype(jnp.bfloat16)
```

```python
import functools

import jax
import jax.numpy as jnp
from jax import lax
from jax.experimental import pallas as pl
from jax.experimental.pallas import tpu as pltpu
from jax.sharding import PartitionSpec as P

BS = 256
CODE = 16
NCHUNK = 4
MESH = pl.DeviceIdType.MESH


def kernel(
    nz, nx, rows,
    a_ref, am_ref, b_ref, bm_ref, c_ref,
    avm, bvm, abuf, bbuf, dense, acc,
    load_sem, ax_send, ay_send, ad_send, a_recv, b_send, b_recv,
):
    z = lax.axis_index("row")
    col = lax.axis_index("col")
    rep = lax.axis_index("rep")
    x = col // 4
    yl = (col // 2) % 2
    core = col % 2
    width = BS
    chunk = b_ref.shape[0] // NCHUNK

    zr, zl = (z + 1) % nz, (z + nz - 1) % nz
    dev_zr, dev_zl = {"row": zr}, {"row": zl}

    def col_of(xx, yy, cc):
        return xx * 4 + yy * 2 + cc

    xs = [x, (x + nx - 1) % nx, (x + 1) % nx, (x + 2) % nx]
    dev_xr = {"col": col_of(xs[2], yl, core)}
    dev_xl = {"col": col_of(xs[1], yl, core)}
    dev_y = [
        {"col": col_of(x, 1 - yl, core), "rep": rep},
        {"col": col_of(x, 1 - yl, core), "rep": 1 - rep},
    ]
    dev_d = {"col": col_of(x, yl, 1 - core)}
    peers = [dev_zr, dev_zl, dev_xr, dev_xl, dev_y[0], dev_y[1], dev_d]

    load_b = [
        pltpu.make_async_copy(
            b_ref.at[pl.ds(j * chunk, chunk), pl.ds(pl.multiple_of(rep * width, width), width)],
            bvm.at[pl.ds(j * chunk, chunk)],
            load_sem.at[j],
        )
        for j in range(NCHUNK)
    ]
    load_a = pltpu.make_async_copy(a_ref, avm, load_sem.at[NCHUNK])
    for copy in load_b:
        copy.start()
    load_a.start()

    barrier = pltpu.get_barrier_semaphore()
    for peer in peers:
        pl.semaphore_signal(barrier, inc=1, device_id=peer, device_id_type=MESH)

    def b_copy(source, j, way, hop):
        piece = bbuf.at[source, pl.ds(j * chunk, chunk)]
        return pltpu.make_async_remote_copy(
            src_ref=piece,
            dst_ref=piece,
            send_sem=b_send.at[way, hop, j],
            recv_sem=b_recv.at[source, j],
            device_id=(dev_zr, dev_zl)[way],
            device_id_type=MESH,
        )

    def a_copy(item, slot, sem, dev):
        piece = abuf.at[2 * item + slot]
        return pltpu.make_async_remote_copy(
            src_ref=piece,
            dst_ref=piece,
            send_sem=sem,
            recv_sem=a_recv.at[2 * item + slot],
            device_id=dev,
            device_id_type=MESH,
        )

    sent = []

    def go(copy):
        copy.start()
        sent.append(copy)

    for j in range(NCHUNK):
        load_b[j].wait()
        keep = jnp.full((chunk, width), bm_ref[(j * chunk) // BS, rep].astype(jnp.float32))
        part = bvm[pl.ds(j * chunk, chunk), :]
        bbuf[z, pl.ds(j * chunk, chunk), :] = part * keep.astype(jnp.bfloat16)

    count = jnp.int32(0)
    lines = lax.broadcasted_iota(jnp.int32, (CODE, BS), 0)
    code = [jnp.zeros((CODE, BS), jnp.float32)] * 2
    weights = []
    for i in range(rows):
        m = am_ref[0, i]
        later = jnp.minimum(count, 1)
        count = count + m
        pair = [jnp.full((CODE, BS), (m * w).astype(jnp.float32)) for w in (1 - later, later)]
        code = [c + jnp.where(lines == i, p, 0.0) for c, p in zip(code, pair)]
        weights.append([p.astype(jnp.bfloat16) for p in pair])
    load_a.wait()

    def pack(t, _):
        at = pl.multiple_of(t * CODE, CODE)
        total = [None, None]
        for i in range(rows):
            part = avm[pl.ds(at + i * BS, CODE), :]
            for slot in range(2):
                term = part * weights[i][slot]
                total[slot] = term if i == 0 else total[slot] + term
        for slot in range(2):
            abuf[2 * col + slot, pl.ds(at, CODE), :] = total[slot]
        return 0

    lax.fori_loop(0, BS // CODE, pack, 0)
    for slot in range(2):
        abuf[2 * col + slot, pl.ds(BS, CODE), :] = code[slot].astype(jnp.bfloat16)

    pl.semaphore_wait(barrier, len(peers))

    def y_send(n, item, slot):
        go(a_copy(item, slot, ay_send.at[2 * n + slot], dev_y[slot]))

    def d_send(n, item, slot):
        go(a_copy(item, slot, ad_send.at[2 * n + slot], dev_d))

    def a_wait(item, slot):
        a_copy(item, slot, ad_send.at[0], dev_d).wait_recv()

    mine = [col_of(xx, yl, core) for xx in xs]
    other = [col_of(xx, 1 - yl, core) for xx in xs]

    def b_step(hop, j):
        if hop < nz // 2 or j < NCHUNK // 2:
            source = (z + nz - hop) % nz
            b_copy(source, j, 0, 0).wait_recv()
            if hop + 1 < nz // 2 or (hop + 1 == nz // 2 and j < NCHUNK // 2):
                go(b_copy(source, j, 0, hop))
        if hop < nz // 2 or j >= NCHUNK // 2:
            source = (z + hop) % nz
            b_copy(source, j, 1, 0).wait_recv()
            if hop + 1 < nz // 2 or (hop + 1 == nz // 2 and j >= NCHUNK // 2):
                go(b_copy(source, j, 1, hop))

    for j in range(NCHUNK):
        go(b_copy(z, j, 0, 0))
        go(b_copy(z, j, 1, 0))
        if j < 2:
            go(a_copy(col, j, ax_send.at[j], dev_xr))
            go(a_copy(col, j, ax_send.at[2 + j], dev_xl))
            y_send(0, col, j)
    for slot in range(2):
        d_send(0, col, slot)

    def x_arrival(slot):
        for n in (1, 2):
            a_wait(mine[n], slot)
            y_send(n, mine[n], slot)
            if slot == n - 1:
                go(a_copy(mine[n], slot, ax_send.at[3 + n], (dev_xr, dev_xl)[slot]))
            d_send(n, mine[n], slot)

    def y_arrival(n, slot):
        a_wait(other[n], slot)
        d_send(4 + n, other[n], slot)

    def expand(xx, yy):
        def body(r, _):
            for cc in range(2):
                k = col_of(xx, yy, cc)
                total = None
                for slot in range(2):
                    row = abuf[2 * k + slot, pl.ds(BS, CODE), :].astype(jnp.float32)
                    at = lax.broadcasted_iota(jnp.int32, (CODE, BS), 0) == r
                    row = jnp.sum(jnp.where(at, row, 0.0), axis=0, keepdims=True)
                    row = jnp.broadcast_to(row, (CODE, BS)).astype(jnp.bfloat16)
                    block = abuf[2 * k + slot, pl.ds(0, BS), :].reshape(BS // CODE, CODE, BS)
                    term = block * row[None]
                    total = term if total is None else total + term
                dense[xx * 2 + yy, pl.ds(pl.multiple_of(r * BS, BS), BS), pl.ds(cc * BS, BS)] = total.reshape(BS, BS)
            return 0

        lax.fori_loop(0, rows, body, 0)

    def d_arrival(n, yy):
        for slot in range(2):
            a_wait(col_of(xs[n], yy, 1 - core), slot)
        expand(xs[n], yy)

    b_step(1, 0)
    x_arrival(0)
    y_arrival(0, 0)
    b_step(1, 1)
    y_arrival(0, 1)
    b_step(1, 2)
    x_arrival(1)
    b_step(1, 3)
    d_arrival(0, yl)
    b_step(2, 0)
    for slot in range(2):
        a_wait(mine[3], slot)
        y_send(3, mine[3], slot)
        d_send(3, mine[3], slot)
    d_arrival(0, 1 - yl)
    y_arrival(1, 0)
    y_arrival(2, 0)
    b_step(2, 1)
    d_arrival(1, yl)
    b_step(2, 2)
    y_arrival(1, 1)
    y_arrival(2, 1)
    d_arrival(2, yl)
    b_step(2, 3)
    d_arrival(3, yl)
    b_step(3, 0)
    for slot in range(2):
        y_arrival(3, slot)
    d_arrival(1, 1 - yl)
    d_arrival(2, 1 - yl)
    b_step(3, 1)
    d_arrival(3, 1 - yl)

    tile = 2 * BS

    def multiply(source, start):
        def body(t, _):
            at = pl.ds(pl.multiple_of(t * tile, tile), tile)
            total = jnp.dot(dense[source, at, :], bbuf[source], preferred_element_type=jnp.float32)
            if start:
                acc[at, :] = total
            else:
                acc[at, :] += total
            return 0

        lax.fori_loop(0, rows * BS // tile, body, 0)

    multiply(z, True)
    multiply((z + 1) % nz, False)
    multiply((z + nz - 1) % nz, False)
    b_step(3, 2)
    multiply((z + 2) % nz, False)
    b_step(3, 3)
    multiply((z + nz - 2) % nz, False)
    multiply((z + 3) % nz, False)
    multiply((z + nz - 3) % nz, False)
    for j in range(NCHUNK):
        b_step(nz // 2, j)
    last = (z + nz // 2) % nz

    def finish(t, _):
        at = pl.ds(pl.multiple_of(t * tile, tile), tile)
        total = jnp.dot(dense[last, at, :], bbuf[last], preferred_element_type=jnp.float32)
        c_ref[at, :] = (acc[at, :] + total).astype(jnp.bfloat16)
        return 0

    lax.fori_loop(0, rows * BS // tile, finish, 0)
    for copy in sent:
        copy.wait_send()


def solution(mesh):
    nz = mesh.shape["row"]
    nx = mesh.shape["col"] // 4

    def per_device(a, am, b, bm):
        rows = am.shape[0]
        ncol = nx * 4
        depth = b.shape[0]
        width = b.shape[1] // 2
        return pl.pallas_call(
            functools.partial(kernel, nz, nx, rows),
            out_shape=jax.ShapeDtypeStruct((a.shape[0], width), jnp.bfloat16),
            in_specs=[
                pl.BlockSpec(memory_space=pltpu.HBM),
                pl.BlockSpec(memory_space=pltpu.SMEM),
                pl.BlockSpec(memory_space=pltpu.HBM),
                pl.BlockSpec(memory_space=pltpu.SMEM),
            ],
            out_specs=pl.BlockSpec(memory_space=pltpu.VMEM),
            scratch_shapes=[
                pltpu.VMEM(a.shape, jnp.bfloat16),
                pltpu.VMEM((depth, width), jnp.bfloat16),
                pltpu.VMEM((2 * ncol, BS + CODE, BS), jnp.bfloat16),
                pltpu.VMEM((nz, depth, width), jnp.bfloat16),
                pltpu.VMEM((nz, a.shape[0], 2 * BS), jnp.bfloat16),
                pltpu.VMEM((a.shape[0], width), jnp.float32),
                pltpu.SemaphoreType.DMA((NCHUNK + 1,)),
                pltpu.SemaphoreType.DMA((6,)),
                pltpu.SemaphoreType.DMA((8,)),
                pltpu.SemaphoreType.DMA((16,)),
                pltpu.SemaphoreType.DMA((2 * ncol,)),
                pltpu.SemaphoreType.DMA((2, 4, NCHUNK)),
                pltpu.SemaphoreType.DMA((nz, NCHUNK)),
            ],
            compiler_params=pltpu.CompilerParams(
                collective_id=0, has_side_effects=True, vmem_limit_bytes=40 * 2**20
            ),
        )(a, am.reshape(1, rows), b, bm)

    spec = P("row", "col")
    return jax.shard_map(
        per_device,
        mesh=mesh,
        in_specs=(spec, spec, spec, spec),
        out_specs=P("row", ("col", "rep")),
        check_vma=False,
    )
```

```python
import functools

import jax
import jax.numpy as jnp
from jax import lax
from jax.experimental import pallas as pl
from jax.experimental.pallas import tpu as pltpu
from jax.sharding import PartitionSpec as P

BS = 256
HALF = BS // 2
TILE = 64
CODE = 16
CHUNKS = ((0, 128), (256, 128), (384, 128), (128, 128))
WAYS = (0, 1, 1, 0)
MESH = pl.DeviceIdType.MESH


def kernel(
    nz, nx, rows,
    a_ref, am_ref, b_ref, bm_ref, c_ref,
    avm, bvm, ams, bms, abuf, bbuf, dense, acc,
    load_sem, ax_send, ay_send, ad_send, a_recv, b_send, b_recv,
):
    z = lax.axis_index("row")
    col = lax.axis_index("col")
    rep = lax.axis_index("rep")
    x = col // 4
    yl = (col // 2) % 2
    core = col % 2
    width = BS
    far = nz // 2

    def col_of(xx, yy, cc):
        return xx * 4 + yy * 2 + cc

    xs = [x, (x + nx - 1) % nx, (x + 1) % nx, (x + 2) % nx]
    dev_z = ({"row": (z + 1) % nz}, {"row": (z + nz - 1) % nz})
    dev_x = ({"col": col_of(xs[2], yl, core)}, {"col": col_of(xs[1], yl, core)})
    dev_y = (
        {"col": col_of(x, 1 - yl, core), "rep": rep},
        {"col": col_of(x, 1 - yl, core), "rep": 1 - rep},
    )
    dev_d = {"col": col_of(x, yl, 1 - core)}
    peers = [*dev_z, *dev_x, *dev_y, dev_d]

    load_bm = pltpu.make_async_copy(bm_ref, bms, load_sem.at[0])
    load_am = pltpu.make_async_copy(am_ref, ams, load_sem.at[1])
    load_b = pltpu.make_async_copy(
        b_ref.at[:, pl.ds(pl.multiple_of(rep * width, width), width)], bvm, load_sem.at[2]
    )
    load_a = pltpu.make_async_copy(a_ref, avm, load_sem.at[3])
    for copy in (load_bm, load_b, load_am, load_a):
        copy.start()

    barrier = pltpu.get_barrier_semaphore()
    for peer in peers:
        pl.semaphore_signal(barrier, inc=1, device_id=peer, device_id_type=MESH)

    sent = []

    def go(copy):
        copy.start()
        sent.append(copy)

    def b_copy(source, j, way, hop):
        piece = bbuf.at[source, pl.ds(*CHUNKS[j])]
        return pltpu.make_async_remote_copy(
            src_ref=piece,
            dst_ref=piece,
            send_sem=b_send.at[way, hop, j],
            recv_sem=b_recv.at[source, j],
            device_id=dev_z[way],
            device_id_type=MESH,
        )

    def a_copy(item, slot, part, sem, dev):
        start, size = ((0, BS + CODE), (0, HALF), (HALF, HALF + CODE))[part]
        piece = abuf.at[2 * item + slot, pl.ds(start, size)]
        return pltpu.make_async_remote_copy(
            src_ref=piece,
            dst_ref=piece,
            send_sem=sem,
            recv_sem=a_recv.at[2 * item + slot, part],
            device_id=dev,
            device_id_type=MESH,
        )

    def b_step(hop, j):
        for way in range(2):
            if hop < far or WAYS[j] == way:
                source = ((z + nz - hop) % nz, (z + hop) % nz)[way]
                b_copy(source, j, way, 0).wait_recv()
                if hop + 1 < far or (hop + 1 == far and WAYS[j] == way):
                    go(b_copy(source, j, way, hop))

    def y_send(n, item, slot, part):
        link = (slot + part) % 2
        go(a_copy(item, slot, part, ay_send.at[4 * n + 2 * slot + part - 1], dev_y[link]))

    def d_send(n, item, slot):
        go(a_copy(item, slot, 0, ad_send.at[2 * n + slot], dev_d))

    def x_send(n, item, slot, part, way):
        go(a_copy(item, slot, part, ax_send.at[way, 4 * n + 2 * slot + part - 1], dev_x[way]))

    load_bm.wait()
    load_b.wait()
    for start, size in CHUNKS:
        keep = jnp.full((size, width), bms[start // BS, rep].astype(jnp.float32))
        bbuf[z, pl.ds(start, size), :] = bvm[pl.ds(start, size), :] * keep.astype(jnp.bfloat16)
    pl.semaphore_wait(barrier, len(peers))
    for j in range(len(CHUNKS)):
        for way in range(2):
            go(b_copy(z, j, way, 0))

    load_am.wait()
    count = jnp.int32(0)
    lines = lax.broadcasted_iota(jnp.int32, (CODE, BS), 0)
    code = [jnp.zeros((CODE, BS), jnp.float32)] * 2
    weights = []
    for i in range(rows):
        m = ams[0, i]
        later = jnp.minimum(count, 1)
        count = count + m
        pair = [jnp.full((CODE, BS), (m * w).astype(jnp.float32)) for w in (1 - later, later)]
        code = [c + jnp.where(lines == i, p, 0.0) for c, p in zip(code, pair)]
        weights.append([p.astype(jnp.bfloat16) for p in pair])
    load_a.wait()

    def pack(t, _):
        at = pl.multiple_of(t * 4 * CODE, 4 * CODE)
        total = [None, None]
        for i in range(rows):
            part = avm[pl.ds(at + i * BS, 4 * CODE), :].reshape(4, CODE, BS)
            for slot in range(2):
                term = part * weights[i][slot][None]
                total[slot] = term if i == 0 else total[slot] + term
        for slot in range(2):
            abuf[2 * col + slot, pl.ds(at, 4 * CODE), :] = total[slot].reshape(4 * CODE, BS)
        return 0

    lax.fori_loop(0, BS // (4 * CODE), pack, 0)
    for slot in range(2):
        abuf[2 * col + slot, pl.ds(BS, CODE), :] = code[slot].astype(jnp.bfloat16)
    for turn in range(4):
        for way in range(2):
            x_send(0, col, (turn // 2 + way) % 2, turn % 2 + 1, way)
        if turn < 2:
            for slot in range(2):
                y_send(0, col, slot, turn + 1)
    for slot in range(2):
        d_send(0, col, slot)

    mine = [col_of(xx, yl, core) for xx in xs]
    other = [col_of(xx, 1 - yl, core) for xx in xs]

    def a_wait(item, slot, part):
        a_copy(item, slot, part, ad_send.at[0], dev_d).wait_recv()

    def x_arrival(turn):
        part = turn % 2 + 1
        for n in (1, 2):
            slot = (turn // 2 + n - 1) % 2
            a_wait(mine[n], slot, part)
            y_send(n, mine[n], slot, part)
            if turn < 2:
                x_send(1, mine[n], slot, part, n - 1)
            if part == 2:
                d_send(n, mine[n], slot)

    def x_second(part):
        for slot in range(2):
            a_wait(mine[3], slot, part)
            if part == 1:
                y_send(3, mine[3], slot, part)
            else:
                d_send(3, mine[3], slot)

    def y_arrival(turn):
        part = turn % 2 + 1
        for n in (1, 2):
            slot = (turn // 2 + n - 1) % 2
            a_wait(other[n], slot, part)
            if part == 2:
                d_send(4 + n, other[n], slot)
                if slot == n - 1:
                    x_send(2, other[n], slot, 2, n - 1)

    def y_plain(n, part):
        for slot in range(2):
            a_wait(other[n], slot, part)
            if part == (1 if n else 2):
                d_send(4 + n, other[n], slot)

    def expand(n, yy):
        xx = xs[n]
        for slot in range(2):
            a_wait(col_of(xx, yy, 1 - core), slot, 0)

        weights = []
        for cc in range(2):
            for slot in range(2):
                line = abuf[2 * col_of(xx, yy, cc) + slot, pl.ds(BS, CODE), :].astype(jnp.float32)
                weights.append(
                    [jnp.broadcast_to(line[r : r + 1], (CODE, BS)).astype(jnp.bfloat16)[None] for r in range(rows)]
                )

        def body(t, _):
            at = pl.multiple_of(t * TILE, TILE)
            for cc in range(2):
                k = col_of(xx, yy, cc)
                one, two = (
                    abuf[2 * k + slot, pl.ds(at, TILE), :].reshape(TILE // CODE, CODE, BS) for slot in range(2)
                )
                for r in range(rows):
                    total = one * weights[2 * cc][r] + two * weights[2 * cc + 1][r]
                    dense[xx * 2 + yy, pl.ds(at + r * BS, TILE), pl.ds(cc * BS, BS)] = total.reshape(TILE, BS)
            return 0

        lax.fori_loop(0, BS // TILE, body, 0)

    def multiply(source, first=False):
        total = jnp.dot(dense[source], bbuf[source], preferred_element_type=jnp.float32)
        acc[...] = total if first else acc[...] + total

    expand(0, yl)
    b_step(1, 0)
    x_arrival(0)
    y_plain(0, 1)
    b_step(1, 1)
    x_arrival(1)
    y_plain(0, 2)
    b_step(1, 2)
    x_arrival(2)
    expand(0, 1 - yl)
    b_step(1, 3)
    y_arrival(0)
    x_arrival(3)
    b_step(2, 0)
    y_arrival(1)
    x_second(1)
    expand(1, yl)
    b_step(2, 1)
    y_arrival(2)
    x_second(2)
    expand(2, yl)
    b_step(2, 2)
    y_arrival(3)
    expand(3, yl)
    b_step(2, 3)
    expand(1, 1 - yl)
    y_plain(3, 2)
    y_plain(3, 1)
    expand(2, 1 - yl)
    b_step(3, 0)
    expand(3, 1 - yl)
    b_step(3, 1)
    multiply(z, True)
    b_step(3, 2)
    multiply((z + 1) % nz)
    b_step(3, 3)
    multiply((z + nz - 1) % nz)
    multiply((z + 2) % nz)
    multiply((z + nz - 2) % nz)
    multiply((z + 3) % nz)
    multiply((z + nz - 3) % nz)
    for j in range(len(CHUNKS)):
        b_step(far, j)
    last = (z + far) % nz
    total = jnp.dot(dense[last], bbuf[last], preferred_element_type=jnp.float32)
    c_ref[...] = (acc[...] + total).astype(jnp.bfloat16)
    for copy in sent:
        copy.wait_send()


def solution(mesh):
    nz = mesh.shape["row"]
    nx = mesh.shape["col"] // 4

    def per_device(a, am, b, bm):
        rows = am.shape[0]
        ncol = nx * 4
        depth = b.shape[0]
        width = b.shape[1] // 2
        am = am.reshape(1, rows)
        return pl.pallas_call(
            functools.partial(kernel, nz, nx, rows),
            out_shape=jax.ShapeDtypeStruct((a.shape[0], width), jnp.bfloat16),
            in_specs=[pl.BlockSpec(memory_space=pl.ANY)] * 4,
            out_specs=pl.BlockSpec(memory_space=pltpu.VMEM),
            scratch_shapes=[
                pltpu.VMEM(a.shape, jnp.bfloat16),
                pltpu.VMEM((depth, width), jnp.bfloat16),
                pltpu.SMEM(am.shape, jnp.int32),
                pltpu.SMEM(bm.shape, jnp.int32),
                pltpu.VMEM((2 * ncol, BS + CODE, BS), jnp.bfloat16),
                pltpu.VMEM((nz, depth, width), jnp.bfloat16),
                pltpu.VMEM((nz, a.shape[0], 2 * BS), jnp.bfloat16),
                pltpu.VMEM((a.shape[0], width), jnp.float32),
                pltpu.SemaphoreType.DMA((4,)),
                pltpu.SemaphoreType.DMA((2, 12)),
                pltpu.SemaphoreType.DMA((16,)),
                pltpu.SemaphoreType.DMA((16,)),
                pltpu.SemaphoreType.DMA((2 * ncol, 3)),
                pltpu.SemaphoreType.DMA((2, nz // 2, len(CHUNKS))),
                pltpu.SemaphoreType.DMA((nz, len(CHUNKS))),
            ],
            compiler_params=pltpu.CompilerParams(
                collective_id=0, has_side_effects=True, vmem_limit_bytes=58 * 2**20
            ),
        )(a, am, b, bm)

    spec = P("row", "col")
    return jax.shard_map(
        per_device,
        mesh=mesh,
        in_specs=(spec, spec, spec, spec),
        out_specs=P("row", ("col", "rep")),
        check_vma=False,
    )
```

```python
import functools

import jax
import jax.numpy as jnp
from jax import lax
from jax.experimental import pallas as pl
from jax.experimental.pallas import tpu as pltpu
from jax.sharding import PartitionSpec as P

BS = 256
HALF = BS // 2
TILE = 64
CODE = 16
CHUNKS = ((0, 128), (256, 128), (384, 128), (128, 128))
WAYS = (0, 1, 1, 0)
X_FIRST, X_FAR, Y_OWN, Y_FIRST, Y_FAR, D_FIRST = 0, 4, 6, 8, 12, 14
MESH = pl.DeviceIdType.MESH


def kernel(
    nz, nx, rows,
    a_ref, am_ref, b_ref, bm_ref, c_ref,
    avm, bvm, ams, bms, abuf, bbuf, dense, acc,
    load_sem, a_send, a_recv, b_send, b_recv,
):
    z = lax.axis_index("row")
    col = lax.axis_index("col")
    rep = lax.axis_index("rep")
    x = col // 4
    yl = (col // 2) % 2
    core = col % 2
    width = BS
    far = nz // 2

    def col_of(xx, yy, cc):
        return xx * 4 + yy * 2 + cc

    xs = [x, (x + nx - 1) % nx, (x + 1) % nx, (x + 2) % nx]
    dev_z = ({"row": (z + 1) % nz}, {"row": (z + nz - 1) % nz})
    dev_x = ({"col": col_of(xs[2], yl, core)}, {"col": col_of(xs[1], yl, core)})
    dev_y = (
        {"col": col_of(x, 1 - yl, core), "rep": rep},
        {"col": col_of(x, 1 - yl, core), "rep": 1 - rep},
    )
    dev_d = {"col": col_of(x, yl, 1 - core)}
    peers = [*dev_z, *dev_x, *dev_y, dev_d]

    load_bm = pltpu.make_async_copy(bm_ref, bms, load_sem.at[0])
    load_am = pltpu.make_async_copy(am_ref, ams, load_sem.at[1])
    load_b = pltpu.make_async_copy(
        b_ref.at[:, pl.ds(pl.multiple_of(rep * width, width), width)], bvm, load_sem.at[2]
    )
    load_a = pltpu.make_async_copy(a_ref, avm, load_sem.at[3])
    for copy in (load_bm, load_b, load_am, load_a):
        copy.start()

    barrier = pltpu.get_barrier_semaphore()
    for peer in peers:
        pl.semaphore_signal(barrier, inc=1, device_id=peer, device_id_type=MESH)

    def remote(piece, send_sem, recv_sem, dev):
        return pltpu.make_async_remote_copy(
            src_ref=piece,
            dst_ref=piece,
            send_sem=send_sem,
            recv_sem=recv_sem,
            device_id=dev,
            device_id_type=MESH,
        )

    def b_send_to(source, j, way, hop):
        sem = b_recv.at[(hop - 1) * len(CHUNKS) + j if hop < far else (far - 1) * len(CHUNKS)]
        remote(bbuf.at[source, pl.ds(*CHUNKS[j])], b_send, sem, dev_z[way]).start()

    def b_wait(sem, lines):
        remote(bbuf.at[z, pl.ds(0, lines)], b_send, sem, dev_z[0]).wait_recv()

    def b_step(hop, j):
        b_wait(b_recv.at[(hop - 1) * len(CHUNKS) + j], 2 * CHUNKS[j][1])
        for way in range(2):
            if hop + 1 < far or WAYS[j] == way:
                b_send_to(((z + nz - hop) % nz, (z + hop) % nz)[way], j, way, hop + 1)

    def a_send_to(item, slot, part, sem, dev):
        start, size = ((0, BS + CODE), (0, HALF), (HALF, HALF + CODE))[part]
        remote(abuf.at[2 * item + slot, pl.ds(start, size)], a_send, a_recv.at[sem], dev).start()

    def y_send(item, slot, part, sem):
        a_send_to(item, slot, part, sem, dev_y[(slot + part) % 2])

    def d_send(n, item, slot):
        a_send_to(item, slot, 0, D_FIRST + n, dev_d)

    def x_send(item, slot, part, way, sem):
        a_send_to(item, slot, part, sem, dev_x[way])

    def a_wait(sem, part):
        b_wait(a_recv.at[sem], 2 * (0, HALF, HALF + CODE)[part])

    load_bm.wait()
    load_b.wait()
    for start, size in CHUNKS:
        keep = jnp.full((size, width), bms[start // BS, rep].astype(jnp.float32))
        bbuf[z, pl.ds(start, size), :] = bvm[pl.ds(start, size), :] * keep.astype(jnp.bfloat16)
    pl.semaphore_wait(barrier, len(peers))
    for j in range(len(CHUNKS)):
        for way in range(2):
            b_send_to(z, j, way, 1)

    load_am.wait()
    count = jnp.int32(0)
    lines = lax.broadcasted_iota(jnp.int32, (CODE, BS), 0)
    code = [jnp.zeros((CODE, BS), jnp.float32)] * 2
    weights = []
    for i in range(rows):
        m = ams[0, i]
        later = jnp.minimum(count, 1)
        count = count + m
        pair = [jnp.full((CODE, BS), (m * w).astype(jnp.float32)) for w in (1 - later, later)]
        code = [c + jnp.where(lines == i, p, 0.0) for c, p in zip(code, pair)]
        weights.append([p.astype(jnp.bfloat16) for p in pair])
    load_a.wait()

    def pack(t, _):
        at = pl.multiple_of(t * 4 * CODE, 4 * CODE)
        total = [None, None]
        for i in range(rows):
            part = avm[pl.ds(at + i * BS, 4 * CODE), :].reshape(4, CODE, BS)
            for slot in range(2):
                term = part * weights[i][slot][None]
                total[slot] = term if i == 0 else total[slot] + term
        for slot in range(2):
            abuf[2 * col + slot, pl.ds(at, 4 * CODE), :] = total[slot].reshape(4 * CODE, BS)
        return 0

    lax.fori_loop(0, BS // (4 * CODE), pack, 0)
    for slot in range(2):
        abuf[2 * col + slot, pl.ds(BS, CODE), :] = code[slot].astype(jnp.bfloat16)
    for turn in range(4):
        for way in range(2):
            x_send(col, (turn // 2 + way) % 2, turn % 2 + 1, way, X_FIRST + turn)
        if turn < 2:
            for slot in range(2):
                y_send(col, slot, turn + 1, Y_OWN + turn)
    for slot in range(2):
        d_send(0, col, slot)

    mine = [col_of(xx, yl, core) for xx in xs]
    other = [col_of(xx, 1 - yl, core) for xx in xs]

    def x_arrival(turn):
        part = turn % 2 + 1
        a_wait(X_FIRST + turn, part)
        for n in (1, 2):
            slot = (turn // 2 + n - 1) % 2
            y_send(mine[n], slot, part, Y_FIRST + turn)
            if turn < 2:
                x_send(mine[n], slot, part, n - 1, X_FAR + turn)
            if part == 2:
                d_send(n, mine[n], slot)

    def x_second(part):
        a_wait(X_FAR + part - 1, part)
        for slot in range(2):
            if part == 1:
                y_send(mine[3], slot, part, Y_FAR)
            else:
                d_send(3, mine[3], slot)

    def y_own():
        for part in (1, 2):
            a_wait(Y_OWN + part - 1, part)
        for slot in range(2):
            d_send(4, other[0], slot)

    def y_arrival(turn):
        part = turn % 2 + 1
        a_wait(Y_FIRST + turn, part)
        if part == 2:
            for n in (1, 2):
                slot = (turn // 2 + n - 1) % 2
                if slot == n - 1:
                    x_send(other[n], slot, part, n - 1, Y_FAR + 1)
                d_send(4 + n, other[n], slot)

    def y_far():
        for part in (2, 1):
            a_wait(Y_FAR + part - 1, part)
        for slot in range(2):
            d_send(7, other[3], slot)

    def expand(n, far_y):
        xx = xs[n]
        yy = 1 - yl if far_y else yl
        remote(abuf.at[pl.ds(0, 2)], a_send, a_recv.at[D_FIRST + n + 4 * far_y], dev_d).wait_recv()

        weights = []
        for cc in range(2):
            for slot in range(2):
                line = abuf[2 * col_of(xx, yy, cc) + slot, pl.ds(BS, CODE), :].astype(jnp.float32)
                weights.append(
                    [jnp.broadcast_to(line[r : r + 1], (CODE, BS)).astype(jnp.bfloat16)[None] for r in range(rows)]
                )

        def body(t, _):
            at = pl.multiple_of(t * TILE, TILE)
            for cc in range(2):
                k = col_of(xx, yy, cc)
                one, two = (
                    abuf[2 * k + slot, pl.ds(at, TILE), :].reshape(TILE // CODE, CODE, BS) for slot in range(2)
                )
                for r in range(rows):
                    total = one * weights[2 * cc][r] + two * weights[2 * cc + 1][r]
                    dense[xx * 2 + yy, pl.ds(at + r * BS, TILE), pl.ds(cc * BS, BS)] = total.reshape(TILE, BS)
            return 0

        lax.fori_loop(0, BS // TILE, body, 0)

    def multiply(source, first=False):
        total = jnp.dot(dense[source], bbuf[source], preferred_element_type=jnp.float32)
        acc[...] = total if first else acc[...] + total

    expand(0, 0)
    b_step(1, 0)
    x_arrival(0)
    b_step(1, 1)
    x_arrival(1)
    y_own()
    b_step(1, 2)
    x_arrival(2)
    expand(0, 1)
    b_step(1, 3)
    y_arrival(0)
    x_arrival(3)
    b_step(2, 0)
    y_arrival(1)
    x_second(1)
    expand(1, 0)
    b_step(2, 1)
    y_arrival(2)
    x_second(2)
    expand(2, 0)
    b_step(2, 2)
    y_arrival(3)
    expand(3, 0)
    b_step(2, 3)
    expand(1, 1)
    y_far()
    expand(2, 1)
    b_step(3, 0)
    expand(3, 1)
    b_step(3, 1)
    multiply(z, True)
    b_step(3, 2)
    multiply((z + 1) % nz)
    b_step(3, 3)
    multiply((z + nz - 1) % nz)
    multiply((z + 2) % nz)
    multiply((z + nz - 2) % nz)
    multiply((z + 3) % nz)
    multiply((z + nz - 3) % nz)
    b_wait(b_recv.at[(far - 1) * len(CHUNKS)], b_ref.shape[0])
    last = (z + far) % nz
    total = jnp.dot(dense[last], bbuf[last], preferred_element_type=jnp.float32)
    c_ref[...] = (acc[...] + total).astype(jnp.bfloat16)
    remote(bbuf.at[pl.ds(0, nz - 1)], b_send, b_recv.at[0], dev_z[0]).wait_send()
    remote(abuf.at[pl.ds(0, 30)], a_send, a_recv.at[0], dev_d).wait_send()


def solution(mesh):
    nz = mesh.shape["row"]
    nx = mesh.shape["col"] // 4

    def per_device(a, am, b, bm):
        rows = am.shape[0]
        ncol = nx * 4
        depth = b.shape[0]
        width = b.shape[1] // 2
        am = am.reshape(1, rows)
        return pl.pallas_call(
            functools.partial(kernel, nz, nx, rows),
            out_shape=jax.ShapeDtypeStruct((a.shape[0], width), jnp.bfloat16),
            in_specs=[pl.BlockSpec(memory_space=pl.ANY)] * 4,
            out_specs=pl.BlockSpec(memory_space=pltpu.VMEM),
            scratch_shapes=[
                pltpu.VMEM(a.shape, jnp.bfloat16),
                pltpu.VMEM((depth, width), jnp.bfloat16),
                pltpu.SMEM(am.shape, jnp.int32),
                pltpu.SMEM(bm.shape, jnp.int32),
                pltpu.VMEM((2 * ncol, BS + CODE, BS), jnp.bfloat16),
                pltpu.VMEM((nz, depth, width), jnp.bfloat16),
                pltpu.VMEM((nz, a.shape[0], 2 * BS), jnp.bfloat16),
                pltpu.VMEM((a.shape[0], width), jnp.float32),
                pltpu.SemaphoreType.DMA((4,)),
                pltpu.SemaphoreType.DMA,
                pltpu.SemaphoreType.DMA((D_FIRST + 8,)),
                pltpu.SemaphoreType.DMA,
                pltpu.SemaphoreType.DMA(((nz // 2 - 1) * len(CHUNKS) + 1,)),
            ],
            compiler_params=pltpu.CompilerParams(
                collective_id=0, has_side_effects=True, vmem_limit_bytes=46 * 2**20
            ),
        )(*(pltpu.with_memory_space_constraint(v, pltpu.HBM) for v in (a, am, b, bm)))

    spec = P("row", "col")
    return jax.shard_map(
        per_device,
        mesh=mesh,
        in_specs=(spec, spec, spec, spec),
        out_specs=P("row", ("col", "rep")),
        check_vma=False,
    )
```

```python
import functools

import jax
import jax.numpy as jnp
from jax import lax
from jax.experimental import pallas as pl
from jax.experimental.pallas import tpu as pltpu
from jax.sharding import PartitionSpec as P

BS = 256
HALF = BS // 2
TILE = 64
CODE = 16
CHUNKS = ((0, 128), (256, 128), (384, 128), (128, 128))
WAYS = (0, 1, 1, 0)
X_FIRST, X_FAR, Y_OWN, Y_FIRST, Y_FAR, D_FIRST = 0, 4, 6, 8, 12, 14
MESH = pl.DeviceIdType.MESH


def kernel(
    nz, nx, rows,
    a_ref, am_ref, b_ref, bm_ref, c_ref,
    avm, bvm, ams, bms, abuf, bbuf, dense, acc,
    load_sem, a_send, a_recv, b_send, b_recv,
):
    z = lax.axis_index("row")
    col = lax.axis_index("col")
    rep = lax.axis_index("rep")
    x = col // 4
    yl = (col // 2) % 2
    core = col % 2
    width = BS
    far = nz // 2

    def col_of(xx, yy, cc):
        return xx * 4 + yy * 2 + cc

    xs = [x, (x + nx - 1) % nx, (x + 1) % nx, (x + 2) % nx]
    dev_z = ({"row": (z + 1) % nz}, {"row": (z + nz - 1) % nz})
    dev_x = ({"col": col_of(xs[2], yl, core)}, {"col": col_of(xs[1], yl, core)})
    dev_y = (
        {"col": col_of(x, 1 - yl, core), "rep": rep},
        {"col": col_of(x, 1 - yl, core), "rep": 1 - rep},
    )
    dev_d = {"col": col_of(x, yl, 1 - core)}
    peers = [*dev_z, *dev_x, *dev_y, dev_d]

    load_bm = pltpu.make_async_copy(bm_ref, bms, load_sem.at[0])
    load_am = pltpu.make_async_copy(am_ref, ams, load_sem.at[1])
    load_b = pltpu.make_async_copy(
        b_ref.at[:, pl.ds(pl.multiple_of(rep * width, width), width)], bvm, load_sem.at[2]
    )
    load_a = pltpu.make_async_copy(a_ref, avm, load_sem.at[3])
    for copy in (load_bm, load_b, load_am, load_a):
        copy.start()

    barrier = pltpu.get_barrier_semaphore()
    for peer in peers:
        pl.semaphore_signal(barrier, inc=1, device_id=peer, device_id_type=MESH)

    def remote(piece, send_sem, recv_sem, dev):
        return pltpu.make_async_remote_copy(
            src_ref=piece,
            dst_ref=piece,
            send_sem=send_sem,
            recv_sem=recv_sem,
            device_id=dev,
            device_id_type=MESH,
        )

    def b_send_to(source, j, way, hop):
        sem = b_recv.at[(hop - 1) * len(CHUNKS) + j if hop < far else (far - 1) * len(CHUNKS)]
        remote(bbuf.at[source, pl.ds(*CHUNKS[j])], b_send, sem, dev_z[way]).start()

    def b_wait(sem, lines):
        remote(bbuf.at[z, pl.ds(0, lines)], b_send, sem, dev_z[0]).wait_recv()

    def b_step(hop, j):
        b_wait(b_recv.at[(hop - 1) * len(CHUNKS) + j], 2 * CHUNKS[j][1])
        for way in range(2):
            if hop + 1 < far or WAYS[j] == way:
                b_send_to(((z + nz - hop) % nz, (z + hop) % nz)[way], j, way, hop + 1)

    def a_send_to(item, slot, part, sem, dev):
        start, size = ((0, BS + CODE), (0, HALF), (HALF, HALF + CODE))[part]
        remote(abuf.at[2 * item + slot, pl.ds(start, size)], a_send, a_recv.at[sem], dev).start()

    def y_send(item, slot, part, sem):
        a_send_to(item, slot, part, sem, dev_y[(slot + part) % 2])

    def d_send(n, item, slot):
        a_send_to(item, slot, 0, D_FIRST + n, dev_d)

    def x_send(item, slot, part, way, sem):
        a_send_to(item, slot, part, sem, dev_x[way])

    def a_wait(sem, part):
        b_wait(a_recv.at[sem], 2 * (0, HALF, HALF + CODE)[part])

    load_bm.wait()
    load_b.wait()
    for start, size in CHUNKS:
        keep = jnp.full((size, width), bms[start // BS, rep].astype(jnp.float32))
        bbuf[z, pl.ds(start, size), :] = bvm[pl.ds(start, size), :] * keep.astype(jnp.bfloat16)
    pl.semaphore_wait(barrier, len(peers))
    for j in range(len(CHUNKS)):
        for way in range(2):
            b_send_to(z, j, way, 1)

    load_am.wait()
    count = jnp.int32(0)
    lines = lax.broadcasted_iota(jnp.int32, (CODE, BS), 0)
    code = [jnp.zeros((CODE, BS), jnp.float32)] * 2
    weights = []
    for i in range(rows):
        m = ams[0, i]
        later = jnp.minimum(count, 1)
        count = count + m
        pair = [jnp.full((CODE, BS), (m * w).astype(jnp.float32)) for w in (1 - later, later)]
        code = [c + jnp.where(lines == i, p, 0.0) for c, p in zip(code, pair)]
        weights.append([p.astype(jnp.bfloat16) for p in pair])
    load_a.wait()

    def pack(t, _):
        at = pl.multiple_of(t * 4 * CODE, 4 * CODE)
        total = [None, None]
        for i in range(rows):
            part = avm[pl.ds(at + i * BS, 4 * CODE), :].reshape(4, CODE, BS)
            for slot in range(2):
                term = part * weights[i][slot][None]
                total[slot] = term if i == 0 else total[slot] + term
        for slot in range(2):
            abuf[2 * col + slot, pl.ds(at, 4 * CODE), :] = total[slot].reshape(4 * CODE, BS)
        return 0

    lax.fori_loop(0, BS // (4 * CODE), pack, 0)
    for slot in range(2):
        abuf[2 * col + slot, pl.ds(BS, CODE), :] = code[slot].astype(jnp.bfloat16)
    for turn in range(4):
        for way in range(2):
            x_send(col, (turn // 2 + way) % 2, turn % 2 + 1, way, X_FIRST + turn)
        if turn < 2:
            for slot in range(2):
                y_send(col, slot, turn + 1, Y_OWN + turn)
    for slot in range(2):
        d_send(0, col, slot)

    mine = [col_of(xx, yl, core) for xx in xs]
    other = [col_of(xx, 1 - yl, core) for xx in xs]

    def x_arrival(turn):
        part = turn % 2 + 1
        a_wait(X_FIRST + turn, part)
        for n in (1, 2):
            slot = (turn // 2 + n - 1) % 2
            y_send(mine[n], slot, part, Y_FIRST + turn)
            if turn < 2:
                x_send(mine[n], slot, part, n - 1, X_FAR + turn)
            if part == 2:
                d_send(n, mine[n], slot)

    def x_second(part):
        a_wait(X_FAR + part - 1, part)
        for slot in range(2):
            if part == 1:
                y_send(mine[3], slot, part, Y_FAR)
            else:
                d_send(3, mine[3], slot)

    def y_own():
        for part in (1, 2):
            a_wait(Y_OWN + part - 1, part)
        for slot in range(2):
            d_send(4, other[0], slot)

    def y_arrival(turn):
        part = turn % 2 + 1
        a_wait(Y_FIRST + turn, part)
        if part == 2:
            for n in (1, 2):
                slot = (turn // 2 + n - 1) % 2
                if slot == n - 1:
                    x_send(other[n], slot, part, n - 1, Y_FAR + 1)
                d_send(4 + n, other[n], slot)

    def y_far():
        for part in (2, 1):
            a_wait(Y_FAR + part - 1, part)
        for slot in range(2):
            d_send(7, other[3], slot)

    def expand(n, far_y):
        xx = xs[n]
        yy = 1 - yl if far_y else yl
        remote(abuf.at[pl.ds(0, 2)], a_send, a_recv.at[D_FIRST + n + 4 * far_y], dev_d).wait_recv()

        weights = []
        for cc in range(2):
            for slot in range(2):
                line = abuf[2 * col_of(xx, yy, cc) + slot, pl.ds(BS, CODE), :].astype(jnp.float32)
                weights.append(
                    [jnp.broadcast_to(line[r : r + 1], (CODE, BS)).astype(jnp.bfloat16)[None] for r in range(rows)]
                )

        def body(t, _):
            at = pl.multiple_of(t * TILE, TILE)
            for cc in range(2):
                k = col_of(xx, yy, cc)
                one, two = (
                    abuf[2 * k + slot, pl.ds(at, TILE), :].reshape(TILE // CODE, CODE, BS) for slot in range(2)
                )
                for r in range(rows):
                    total = one * weights[2 * cc][r] + two * weights[2 * cc + 1][r]
                    dense[xx * 2 + yy, pl.ds(at + r * BS, TILE), pl.ds(cc * BS, BS)] = total.reshape(TILE, BS)
            return 0

        lax.fori_loop(0, BS // TILE, body, 0)

    def multiply(panels, hops, panels_before=0, hops_before=0):
        def body(i, _):
            source = (z + nz + i - hops) % nz
            n = (source // 2 + nx - x) % nx
            near = jnp.where(source % 2 == yl, 1, 0)
            place = jnp.where(n == 0, 1 - near, jnp.where(n == nx - 1, 0, n) + 5 - 3 * near)
            far_off = jnp.abs(i - hops)
            ready = place < panels
            done = (far_off <= hops_before) & (place < panels_before)

            @pl.when(ready & jnp.logical_not(done))
            def _():
                acc[...] += jnp.dot(dense[source], bbuf[source], preferred_element_type=jnp.float32)

            return 0

        lax.fori_loop(0, 2 * hops + 1, body, 0)

    acc[...] = jnp.zeros_like(acc)
    expand(0, 0)
    b_step(1, 0)
    x_arrival(0)
    b_step(1, 1)
    x_arrival(1)
    y_own()
    b_step(1, 2)
    x_arrival(2)
    expand(0, 1)
    b_step(1, 3)
    y_arrival(0)
    x_arrival(3)
    multiply(2, 1, 0, 0)
    b_step(2, 0)
    y_arrival(1)
    x_second(1)
    expand(1, 0)
    b_step(2, 1)
    y_arrival(2)
    x_second(2)
    expand(2, 0)
    multiply(4, 1, 2, 1)
    b_step(2, 2)
    y_arrival(3)
    b_step(2, 3)
    y_far()
    expand(3, 0)
    expand(1, 1)
    b_step(3, 0)
    expand(2, 1)
    multiply(7, 2, 4, 1)
    expand(3, 1)
    b_step(3, 1)
    b_step(3, 2)
    multiply(8, 2, 7, 2)
    b_step(3, 3)
    multiply(8, 3, 8, 2)
    b_wait(b_recv.at[(far - 1) * len(CHUNKS)], b_ref.shape[0])
    last = (z + far) % nz
    total = jnp.dot(dense[last], bbuf[last], preferred_element_type=jnp.float32)
    c_ref[...] = (acc[...] + total).astype(jnp.bfloat16)
    remote(bbuf.at[pl.ds(0, nz - 1)], b_send, b_recv.at[0], dev_z[0]).wait_send()
    remote(abuf.at[pl.ds(0, 30)], a_send, a_recv.at[0], dev_d).wait_send()


def solution(mesh):
    nz = mesh.shape["row"]
    nx = mesh.shape["col"] // 4

    def per_device(a, am, b, bm):
        rows = am.shape[0]
        ncol = nx * 4
        depth = b.shape[0]
        width = b.shape[1] // 2
        am = am.reshape(1, rows)
        return pl.pallas_call(
            functools.partial(kernel, nz, nx, rows),
            out_shape=jax.ShapeDtypeStruct((a.shape[0], width), jnp.bfloat16),
            in_specs=[pl.BlockSpec(memory_space=pl.ANY)] * 4,
            out_specs=pl.BlockSpec(memory_space=pltpu.VMEM),
            scratch_shapes=[
                pltpu.VMEM(a.shape, jnp.bfloat16),
                pltpu.VMEM((depth, width), jnp.bfloat16),
                pltpu.SMEM(am.shape, jnp.int32),
                pltpu.SMEM(bm.shape, jnp.int32),
                pltpu.VMEM((2 * ncol, BS + CODE, BS), jnp.bfloat16),
                pltpu.VMEM((nz, depth, width), jnp.bfloat16),
                pltpu.VMEM((nz, a.shape[0], 2 * BS), jnp.bfloat16),
                pltpu.VMEM((a.shape[0], width), jnp.float32),
                pltpu.SemaphoreType.DMA((4,)),
                pltpu.SemaphoreType.DMA,
                pltpu.SemaphoreType.DMA((D_FIRST + 8,)),
                pltpu.SemaphoreType.DMA,
                pltpu.SemaphoreType.DMA(((nz // 2 - 1) * len(CHUNKS) + 1,)),
            ],
            compiler_params=pltpu.CompilerParams(
                collective_id=0, has_side_effects=True, vmem_limit_bytes=46 * 2**20
            ),
        )(*(pltpu.with_memory_space_constraint(v, pltpu.HBM) for v in (a, am, b, bm)))

    spec = P("row", "col")
    return jax.shard_map(
        per_device,
        mesh=mesh,
        in_specs=(spec, spec, spec, spec),
        out_specs=P("row", ("col", "rep")),
        check_vma=False,
    )
```

```python
import functools

import jax
import jax.numpy as jnp
from jax import lax
from jax.experimental import pallas as pl
from jax.experimental.pallas import tpu as pltpu
from jax.sharding import PartitionSpec as P

BS = 256
HALF = BS // 2
TILE = 64
CODE = 16
CHUNKS = ((0, 128), (256, 128), (384, 128), (128, 128))
WAYS = (0, 1, 1, 0)
X_FIRST, X_FAR, Y_OWN, Y_FIRST, Y_FAR, D_FIRST = 0, 4, 6, 8, 12, 14
MESH = pl.DeviceIdType.MESH


def kernel(
    nz, nx, rows,
    a_ref, am_ref, b_ref, bm_ref, c_ref,
    avm, bvm, ams, bms, abuf, bbuf, dense, acc,
    load_sem, a_send, a_recv, b_send, b_recv,
):
    z = lax.axis_index("row")
    col = lax.axis_index("col")
    rep = lax.axis_index("rep")
    x = col // 4
    yl = (col // 2) % 2
    core = col % 2
    width = BS
    far = nz // 2

    def col_of(xx, yy, cc):
        return xx * 4 + yy * 2 + cc

    xs = [x, (x + nx - 1) % nx, (x + 1) % nx, (x + 2) % nx]
    dev_z = ({"row": (z + 1) % nz}, {"row": (z + nz - 1) % nz})
    dev_x = ({"col": col_of(xs[2], yl, core)}, {"col": col_of(xs[1], yl, core)})
    dev_y = (
        {"col": col_of(x, 1 - yl, core), "rep": rep},
        {"col": col_of(x, 1 - yl, core), "rep": 1 - rep},
    )
    dev_d = {"col": col_of(x, yl, 1 - core)}
    peers = [*dev_z, *dev_x, *dev_y, dev_d]

    load_bm = pltpu.make_async_copy(bm_ref, bms, load_sem.at[0])
    load_am = pltpu.make_async_copy(am_ref, ams, load_sem.at[1])
    load_b = pltpu.make_async_copy(
        b_ref.at[:, pl.ds(pl.multiple_of(rep * width, width), width)], bvm, load_sem.at[2]
    )
    load_a = pltpu.make_async_copy(a_ref, avm, load_sem.at[3])
    for copy in (load_bm, load_b, load_am, load_a):
        copy.start()

    barrier = pltpu.get_barrier_semaphore()
    for peer in peers:
        pl.semaphore_signal(barrier, inc=1, device_id=peer, device_id_type=MESH)

    def remote(piece, send_sem, recv_sem, dev):
        return pltpu.make_async_remote_copy(
            src_ref=piece,
            dst_ref=piece,
            send_sem=send_sem,
            recv_sem=recv_sem,
            device_id=dev,
            device_id_type=MESH,
        )

    first = jnp.where((z + nz // 4) % nz < nz // 2, 1, 0)
    second = 1 - first

    def b_send_to(source, j, way, hop):
        sem = b_recv.at[way, (hop - 1) * len(CHUNKS) + j] if hop < far else b_recv.at[0, (far - 1) * len(CHUNKS)]
        dev = {"row": (z + nz + 1 - 2 * way) % nz}
        remote(bbuf.at[source, pl.ds(*CHUNKS[j])], b_send, sem, dev).start()

    def b_wait(sem, lines):
        remote(bbuf.at[z, pl.ds(0, lines)], b_send, sem, dev_z[0]).wait_recv()

    def b_half(way, hop, j):
        b_wait(b_recv.at[way, (hop - 1) * len(CHUNKS) + j], CHUNKS[j][1])
        onward = functools.partial(b_send_to, (z + nz + (2 * way - 1) * hop) % nz, j, way, hop + 1)
        if hop + 1 < far:
            onward()
        else:
            to = (z + nz + 1 - 2 * way) % nz
            takes = WAYS[j]
            takes = jnp.where(((to == 0)), 1, takes)
            takes = jnp.where(((to == 3)), 0, takes)
            pl.when(way == takes)(onward)

    def b_step(hop, j):
        b_half(first, hop, j)
        b_half(second, hop, j)

    def a_send_to(item, slot, part, sem, dev):
        start, size = ((0, BS + CODE), (0, HALF), (HALF, HALF + CODE))[part]
        remote(abuf.at[2 * item + slot, pl.ds(start, size)], a_send, a_recv.at[sem], dev).start()

    def y_send(item, slot, part, sem):
        a_send_to(item, slot, part, sem, dev_y[(slot + part) % 2])

    def d_send(n, item, slot):
        a_send_to(item, slot, 0, D_FIRST + n, dev_d)

    def x_send(item, slot, part, way, sem):
        a_send_to(item, slot, part, sem, dev_x[way])

    def a_wait(sem, part):
        b_wait(a_recv.at[sem], 2 * (0, HALF, HALF + CODE)[part])

    load_bm.wait()
    load_b.wait()
    for start, size in CHUNKS:
        keep = jnp.full((size, width), bms[start // BS, rep].astype(jnp.float32))
        bbuf[z, pl.ds(start, size), :] = bvm[pl.ds(start, size), :] * keep.astype(jnp.bfloat16)
    pl.semaphore_wait(barrier, len(peers))
    for j in range(len(CHUNKS)):
        for way in range(2):
            b_send_to(z, j, way, 1)

    load_am.wait()
    count = jnp.int32(0)
    lines = lax.broadcasted_iota(jnp.int32, (CODE, BS), 0)
    code = [jnp.zeros((CODE, BS), jnp.float32)] * 2
    weights = []
    for i in range(rows):
        m = ams[0, i]
        later = jnp.minimum(count, 1)
        count = count + m
        pair = [jnp.full((CODE, BS), (m * w).astype(jnp.float32)) for w in (1 - later, later)]
        code = [c + jnp.where(lines == i, p, 0.0) for c, p in zip(code, pair)]
        weights.append([p.astype(jnp.bfloat16) for p in pair])
    load_a.wait()

    def pack(t, _):
        at = pl.multiple_of(t * 4 * CODE, 4 * CODE)
        total = [None, None]
        for i in range(rows):
            part = avm[pl.ds(at + i * BS, 4 * CODE), :].reshape(4, CODE, BS)
            for slot in range(2):
                term = part * weights[i][slot][None]
                total[slot] = term if i == 0 else total[slot] + term
        for slot in range(2):
            abuf[2 * col + slot, pl.ds(at, 4 * CODE), :] = total[slot].reshape(4 * CODE, BS)
        return 0

    lax.fori_loop(0, BS // (4 * CODE), pack, 0)
    for slot in range(2):
        abuf[2 * col + slot, pl.ds(BS, CODE), :] = code[slot].astype(jnp.bfloat16)
    for turn in range(4):
        for way in range(2):
            x_send(col, (turn // 2 + way) % 2, turn % 2 + 1, way, X_FIRST + turn)
        if turn < 2:
            for slot in range(2):
                y_send(col, slot, turn + 1, Y_OWN + turn)
    for slot in range(2):
        d_send(0, col, slot)

    mine = [col_of(xx, yl, core) for xx in xs]
    other = [col_of(xx, 1 - yl, core) for xx in xs]

    def x_arrival(turn):
        part = turn % 2 + 1
        a_wait(X_FIRST + turn, part)
        for n in (1, 2):
            slot = (turn // 2 + n - 1) % 2
            y_send(mine[n], slot, part, Y_FIRST + turn)
            if turn < 2:
                x_send(mine[n], slot, part, n - 1, X_FAR + turn)
            if part == 2:
                d_send(n, mine[n], slot)

    def x_second(part):
        a_wait(X_FAR + part - 1, part)
        for slot in range(2):
            if part == 1:
                y_send(mine[3], slot, part, Y_FAR)
            else:
                d_send(3, mine[3], slot)

    def y_own():
        for part in (1, 2):
            a_wait(Y_OWN + part - 1, part)
        for slot in range(2):
            d_send(4, other[0], slot)

    def y_arrival(turn):
        part = turn % 2 + 1
        a_wait(Y_FIRST + turn, part)
        if part == 2:
            for n in (1, 2):
                slot = (turn // 2 + n - 1) % 2
                if slot == n - 1:
                    x_send(other[n], slot, part, n - 1, Y_FAR + 1)
                d_send(4 + n, other[n], slot)

    def y_far():
        for part in (2, 1):
            a_wait(Y_FAR + part - 1, part)
        for slot in range(2):
            d_send(7, other[3], slot)

    def expand(n, far_y):
        xx = xs[n]
        yy = 1 - yl if far_y else yl
        remote(abuf.at[pl.ds(0, 2)], a_send, a_recv.at[D_FIRST + n + 4 * far_y], dev_d).wait_recv()

        weights = []
        for cc in range(2):
            for slot in range(2):
                line = abuf[2 * col_of(xx, yy, cc) + slot, pl.ds(BS, CODE), :].astype(jnp.float32)
                weights.append(
                    [jnp.broadcast_to(line[r : r + 1], (CODE, BS)).astype(jnp.bfloat16)[None] for r in range(rows)]
                )

        def body(t, _):
            at = pl.multiple_of(t * TILE, TILE)
            for cc in range(2):
                k = col_of(xx, yy, cc)
                one, two = (
                    abuf[2 * k + slot, pl.ds(at, TILE), :].reshape(TILE // CODE, CODE, BS) for slot in range(2)
                )
                for r in range(rows):
                    total = one * weights[2 * cc][r] + two * weights[2 * cc + 1][r]
                    dense[xx * 2 + yy, pl.ds(at + r * BS, TILE), pl.ds(cc * BS, BS)] = total.reshape(TILE, BS)
            return 0

        lax.fori_loop(0, BS // TILE, body, 0)

    def multiply(panels, hops, panels_before=0, hops_before=0):
        def body(i, _):
            source = (z + nz + i - hops) % nz
            n = (source // 2 + nx - x) % nx
            near = jnp.where(source % 2 == yl, 1, 0)
            place = jnp.where(n == 0, 1 - near, jnp.where(n == nx - 1, 0, n) + 5 - 3 * near)
            far_off = jnp.abs(i - hops)
            ready = place < panels
            done = (far_off <= hops_before) & (place < panels_before)

            @pl.when(ready & jnp.logical_not(done))
            def _():
                acc[...] += jnp.dot(dense[source], bbuf[source], preferred_element_type=jnp.float32)

            return 0

        lax.fori_loop(0, 2 * hops + 1, body, 0)

    acc[...] = jnp.zeros_like(acc)
    expand(0, 0)
    b_half(first, 1, 0)
    b_half(first, 1, 1)
    b_half(second, 1, 0)
    x_arrival(0)
    b_half(first, 1, 2)
    b_half(second, 1, 1)
    x_arrival(1)
    y_own()
    b_half(first, 1, 3)
    b_half(second, 1, 2)
    x_arrival(2)
    expand(0, 1)
    b_half(first, 2, 0)
    b_half(second, 1, 3)
    y_arrival(0)
    x_arrival(3)
    multiply(2, 1, 0, 0)
    b_half(first, 2, 1)
    b_half(second, 2, 0)
    y_arrival(1)
    x_second(1)
    expand(1, 0)
    b_half(first, 2, 2)
    b_half(second, 2, 1)
    y_arrival(2)
    x_second(2)
    expand(2, 0)
    multiply(4, 1, 2, 1)
    b_half(first, 2, 3)
    b_half(second, 2, 2)
    y_arrival(3)
    b_half(first, 3, 0)
    b_half(second, 2, 3)
    y_far()
    expand(3, 0)
    expand(1, 1)
    b_half(first, 3, 1)
    b_half(second, 3, 0)
    expand(2, 1)
    multiply(7, 2, 4, 1)
    expand(3, 1)
    b_half(first, 3, 2)
    b_half(second, 3, 1)
    b_half(first, 3, 3)
    b_half(second, 3, 2)
    multiply(8, 2, 7, 2)
    b_half(second, 3, 3)
    multiply(8, 3, 8, 2)
    b_wait(b_recv.at[0, (far - 1) * len(CHUNKS)], b_ref.shape[0])
    last = (z + far) % nz
    total = jnp.dot(dense[last], bbuf[last], preferred_element_type=jnp.float32)
    c_ref[...] = (acc[...] + total).astype(jnp.bfloat16)
    remote(bbuf.at[pl.ds(0, nz - 2)], b_send, b_recv.at[0, 0], dev_z[0]).wait_send()
    pl.when(((z == 4) | (z == 7)))(remote(bbuf.at[0, pl.ds(0, BS)], b_send, b_recv.at[0, 0], dev_z[0]).wait_send)
    pl.when(((z == 0) | (z == 3) | (z == 5) | (z == 6)))(remote(bbuf.at[pl.ds(0, 1)], b_send, b_recv.at[0, 0], dev_z[0]).wait_send)
    pl.when(((z == 1) | (z == 2)))(remote(abuf.at[0, pl.ds(0, BS)], b_send, b_recv.at[0, 0], dev_z[0]).wait_send)
    pl.when(((z == 1) | (z == 2)))(remote(bbuf.at[pl.ds(0, 1)], b_send, b_recv.at[0, 0], dev_z[0]).wait_send)
    remote(abuf.at[pl.ds(0, 30)], a_send, a_recv.at[0], dev_d).wait_send()


def solution(mesh):
    nz = mesh.shape["row"]
    nx = mesh.shape["col"] // 4

    def per_device(a, am, b, bm):
        rows = am.shape[0]
        ncol = nx * 4
        depth = b.shape[0]
        width = b.shape[1] // 2
        am = am.reshape(1, rows)
        return pl.pallas_call(
            functools.partial(kernel, nz, nx, rows),
            out_shape=jax.ShapeDtypeStruct((a.shape[0], width), jnp.bfloat16),
            in_specs=[pl.BlockSpec(memory_space=pl.ANY)] * 4,
            out_specs=pl.BlockSpec(memory_space=pltpu.VMEM),
            scratch_shapes=[
                pltpu.VMEM(a.shape, jnp.bfloat16),
                pltpu.VMEM((depth, width), jnp.bfloat16),
                pltpu.SMEM(am.shape, jnp.int32),
                pltpu.SMEM(bm.shape, jnp.int32),
                pltpu.VMEM((2 * ncol, BS + CODE, BS), jnp.bfloat16),
                pltpu.VMEM((nz, depth, width), jnp.bfloat16),
                pltpu.VMEM((nz, a.shape[0], 2 * BS), jnp.bfloat16),
                pltpu.VMEM((a.shape[0], width), jnp.float32),
                pltpu.SemaphoreType.DMA((4,)),
                pltpu.SemaphoreType.DMA,
                pltpu.SemaphoreType.DMA((D_FIRST + 8,)),
                pltpu.SemaphoreType.DMA,
                pltpu.SemaphoreType.DMA((2, (nz // 2 - 1) * len(CHUNKS) + 1)),
            ],
            compiler_params=pltpu.CompilerParams(
                collective_id=0, has_side_effects=True, vmem_limit_bytes=46 * 2**20
            ),
        )(*(pltpu.with_memory_space_constraint(v, pltpu.HBM) for v in (a, am, b, bm)))

    spec = P("row", "col")
    return jax.shard_map(
        per_device,
        mesh=mesh,
        in_specs=(spec, spec, spec, spec),
        out_specs=P("row", ("col", "rep")),
        check_vma=False,
    )
```

```python
import functools

import jax
import jax.numpy as jnp
from jax import lax
from jax.experimental import pallas as pl
from jax.experimental.pallas import tpu as pltpu
from jax.sharding import PartitionSpec as P

BS = 256
HALF = BS // 2
TILE = 64
CODE = 16
CHUNKS = ((0, 128), (256, 128), (384, 128), (128, 128))
WAYS = (0, 1, 1, 0)
X_FIRST, X_FAR, Y_OWN, Y_FIRST, Y_FAR, D_FIRST = 0, 4, 6, 8, 12, 14
MESH = pl.DeviceIdType.MESH


def kernel(
    nz, nx, rows,
    a_ref, am_ref, b_ref, bm_ref, c_ref,
    avm, bvm, ams, bms, abuf, bbuf, dense, acc,
    load_sem, a_send, a_recv, b_send, b_recv,
):
    z = lax.axis_index("row")
    col = lax.axis_index("col")
    rep = lax.axis_index("rep")
    x = col // 4
    yl = (col // 2) % 2
    core = col % 2
    width = BS
    far = nz // 2

    def col_of(xx, yy, cc):
        return xx * 4 + yy * 2 + cc

    xs = [x, (x + nx - 1) % nx, (x + 1) % nx, (x + 2) % nx]
    dev_z = ({"row": (z + 1) % nz}, {"row": (z + nz - 1) % nz})
    dev_x = ({"col": col_of(xs[2], yl, core)}, {"col": col_of(xs[1], yl, core)})
    dev_y = (
        {"col": col_of(x, 1 - yl, core), "rep": rep},
        {"col": col_of(x, 1 - yl, core), "rep": 1 - rep},
    )
    dev_d = {"col": col_of(x, yl, 1 - core)}
    peers = [*dev_z, *dev_x, *dev_y, dev_d]

    load_bm = pltpu.make_async_copy(bm_ref, bms, load_sem.at[0])
    load_am = pltpu.make_async_copy(am_ref, ams, load_sem.at[1])
    load_b = pltpu.make_async_copy(
        b_ref.at[:, pl.ds(pl.multiple_of(rep * width, width), width)], bvm, load_sem.at[2]
    )
    load_a = pltpu.make_async_copy(a_ref, avm, load_sem.at[3])
    for copy in (load_bm, load_b, load_am, load_a):
        copy.start()

    barrier = pltpu.get_barrier_semaphore()
    for peer in peers:
        pl.semaphore_signal(barrier, inc=1, device_id=peer, device_id_type=MESH)

    def remote(piece, send_sem, recv_sem, dev):
        return pltpu.make_async_remote_copy(
            src_ref=piece,
            dst_ref=piece,
            send_sem=send_sem,
            recv_sem=recv_sem,
            device_id=dev,
            device_id_type=MESH,
        )

    first = jnp.where((z + nz // 4) % nz < nz // 2, 1, 0)
    second = 1 - first

    def b_send_to(source, j, way, hop):
        sem = b_recv.at[way, (hop - 1) * len(CHUNKS) + j] if hop < far else b_recv.at[0, (far - 1) * len(CHUNKS)]
        dev = {"row": (z + nz + 1 - 2 * way) % nz}
        remote(bbuf.at[source, pl.ds(*CHUNKS[j])], b_send, sem, dev).start()

    def b_wait(sem, lines):
        remote(bbuf.at[z, pl.ds(0, lines)], b_send, sem, dev_z[0]).wait_recv()

    def b_half(way, hop, j):
        b_wait(b_recv.at[way, (hop - 1) * len(CHUNKS) + j], CHUNKS[j][1])
        onward = functools.partial(b_send_to, (z + nz + (2 * way - 1) * hop) % nz, j, way, hop + 1)
        if hop + 1 < far:
            onward()
        else:
            to = (z + nz + 1 - 2 * way) % nz
            takes = WAYS[j]
            takes = jnp.where(((to == 0)), 1, takes)
            takes = jnp.where(((to == 3)), 0, takes)
            pl.when(way == takes)(onward)

    def b_step(hop, j):
        b_half(first, hop, j)
        b_half(second, hop, j)

    def a_send_to(item, slot, part, sem, dev):
        start, size = ((0, BS + CODE), (0, HALF), (HALF, HALF + CODE))[part]
        remote(abuf.at[2 * item + slot, pl.ds(start, size)], a_send, a_recv.at[sem], dev).start()

    def y_send(item, slot, part, sem):
        a_send_to(item, slot, part, sem, dev_y[(slot + part) % 2])

    def d_send(n, item, slot):
        a_send_to(item, slot, 0, D_FIRST + n, dev_d)

    def x_send(item, slot, part, way, sem):
        a_send_to(item, slot, part, sem, dev_x[way])

    def a_wait(sem, part):
        b_wait(a_recv.at[sem], 2 * (0, HALF, HALF + CODE)[part])

    acc[...] = jnp.zeros_like(acc)
    load_bm.wait()
    load_b.wait()
    for start, size in CHUNKS:
        keep = jnp.full((size, width), bms[start // BS, rep].astype(jnp.float32))
        bbuf[z, pl.ds(start, size), :] = bvm[pl.ds(start, size), :] * keep.astype(jnp.bfloat16)
    pl.semaphore_wait(barrier, len(peers))
    for j in range(len(CHUNKS)):
        for way in range(2):
            b_send_to(z, j, way, 1)

    load_am.wait()
    count = jnp.int32(0)
    lines = lax.broadcasted_iota(jnp.int32, (CODE, BS), 0)
    code = [jnp.zeros((CODE, BS), jnp.float32)] * 2
    weights = []
    for i in range(rows):
        m = ams[0, i]
        later = jnp.minimum(count, 1)
        count = count + m
        pair = [jnp.full((CODE, BS), (m * w).astype(jnp.float32)) for w in (1 - later, later)]
        code = [c + jnp.where(lines == i, p, 0.0) for c, p in zip(code, pair)]
        weights.append([p.astype(jnp.bfloat16) for p in pair])
    load_a.wait()

    def pack(t, _):
        at = pl.multiple_of(t * 4 * CODE, 4 * CODE)
        total = [None, None]
        for i in range(rows):
            part = avm[pl.ds(at + i * BS, 4 * CODE), :].reshape(4, CODE, BS)
            for slot in range(2):
                term = part * weights[i][slot][None]
                total[slot] = term if i == 0 else total[slot] + term
        for slot in range(2):
            abuf[2 * col + slot, pl.ds(at, 4 * CODE), :] = total[slot].reshape(4 * CODE, BS)
        return 0

    lax.fori_loop(0, BS // (4 * CODE), pack, 0)
    for slot in range(2):
        abuf[2 * col + slot, pl.ds(BS, CODE), :] = code[slot].astype(jnp.bfloat16)
    for turn in range(4):
        for way in range(2):
            x_send(col, (turn // 2 + way) % 2, turn % 2 + 1, way, X_FIRST + turn)
        if turn < 2:
            for slot in range(2):
                y_send(col, slot, turn + 1, Y_OWN + turn)
    for slot in range(2):
        d_send(0, col, slot)

    mine = [col_of(xx, yl, core) for xx in xs]
    other = [col_of(xx, 1 - yl, core) for xx in xs]

    def x_arrival(turn):
        part = turn % 2 + 1
        a_wait(X_FIRST + turn, part)
        for n in (1, 2):
            slot = (turn // 2 + n - 1) % 2
            y_send(mine[n], slot, part, Y_FIRST + turn)
            if turn < 2:
                x_send(mine[n], slot, part, n - 1, X_FAR + turn)
            if part == 2:
                d_send(n, mine[n], slot)

    def x_second(part):
        a_wait(X_FAR + part - 1, part)
        for slot in range(2):
            if part == 1:
                y_send(mine[3], slot, part, Y_FAR)
            else:
                d_send(3, mine[3], slot)

    def y_own():
        for part in (1, 2):
            a_wait(Y_OWN + part - 1, part)
        for slot in range(2):
            d_send(4, other[0], slot)

    def y_arrival(turn):
        part = turn % 2 + 1
        a_wait(Y_FIRST + turn, part)
        if part == 2:
            for n in (1, 2):
                slot = (turn // 2 + n - 1) % 2
                if slot == n - 1:
                    x_send(other[n], slot, part, n - 1, Y_FAR + 1)
                d_send(4 + n, other[n], slot)

    def y_far():
        for part in (2, 1):
            a_wait(Y_FAR + part - 1, part)
        for slot in range(2):
            d_send(7, other[3], slot)

    def expand(n, far_y):
        xx = xs[n]
        yy = 1 - yl if far_y else yl
        remote(abuf.at[pl.ds(0, 2)], a_send, a_recv.at[D_FIRST + n + 4 * far_y], dev_d).wait_recv()

        weights = []
        for cc in range(2):
            for slot in range(2):
                line = abuf[2 * col_of(xx, yy, cc) + slot, pl.ds(BS, CODE), :].astype(jnp.float32)
                weights.append(
                    [jnp.broadcast_to(line[r : r + 1], (CODE, BS)).astype(jnp.bfloat16)[None] for r in range(rows)]
                )

        def body(t, _):
            at = pl.multiple_of(t * TILE, TILE)
            for cc in range(2):
                k = col_of(xx, yy, cc)
                one, two = (
                    abuf[2 * k + slot, pl.ds(at, TILE), :].reshape(TILE // CODE, CODE, BS) for slot in range(2)
                )
                for r in range(rows):
                    total = one * weights[2 * cc][r] + two * weights[2 * cc + 1][r]
                    dense[xx * 2 + yy, pl.ds(at + r * BS, TILE), pl.ds(cc * BS, BS)] = total.reshape(TILE, BS)
            return 0

        lax.fori_loop(0, BS // TILE, body, 0)

    def multiply(panels, hops, panels_before=0, hops_before=0):
        def body(i, _):
            source = (z + nz + i - hops) % nz
            n = (source // 2 + nx - x) % nx
            near = jnp.where(source % 2 == yl, 1, 0)
            place = jnp.where(n == 0, 1 - near, jnp.where(n == nx - 1, 0, n) + 5 - 3 * near)
            far_off = jnp.abs(i - hops)
            ready = place < panels
            done = (far_off <= hops_before) & (place < panels_before)

            @pl.when(ready & jnp.logical_not(done))
            def _():
                acc[...] += jnp.dot(dense[source], bbuf[source], preferred_element_type=jnp.float32)

            return 0

        lax.fori_loop(0, 2 * hops + 1, body, 0)

    expand(0, 0)
    b_half(first, 1, 0)
    b_half(first, 1, 1)
    b_half(second, 1, 0)
    x_arrival(0)
    b_half(first, 1, 2)
    b_half(second, 1, 1)
    x_arrival(1)
    y_own()
    b_half(first, 1, 3)
    b_half(second, 1, 2)
    x_arrival(2)
    expand(0, 1)
    b_half(first, 2, 0)
    b_half(second, 1, 3)
    y_arrival(0)
    x_arrival(3)
    multiply(2, 1, 0, 0)
    b_half(first, 2, 1)
    b_half(second, 2, 0)
    y_arrival(1)
    x_second(1)
    expand(1, 0)
    b_half(first, 2, 2)
    b_half(second, 2, 1)
    y_arrival(2)
    x_second(2)
    expand(2, 0)
    multiply(4, 1, 2, 1)
    b_half(first, 2, 3)
    b_half(second, 2, 2)
    y_arrival(3)
    expand(3, 0)
    b_half(first, 3, 0)
    b_half(second, 2, 3)
    multiply(5, 2, 4, 1)
    y_far()
    expand(1, 1)
    b_half(first, 3, 1)
    b_half(second, 3, 0)
    expand(2, 1)
    multiply(7, 2, 5, 2)
    expand(3, 1)
    b_half(first, 3, 2)
    b_half(second, 3, 1)
    b_half(first, 3, 3)
    b_half(second, 3, 2)
    multiply(8, 2, 7, 2)
    b_half(second, 3, 3)
    multiply(8, 3, 8, 2)
    b_wait(b_recv.at[0, (far - 1) * len(CHUNKS)], b_ref.shape[0])
    last = (z + far) % nz
    total = jnp.dot(dense[last], bbuf[last], preferred_element_type=jnp.float32)
    c_ref[...] = (acc[...] + total).astype(jnp.bfloat16)
    remote(bbuf.at[pl.ds(0, nz - 2)], b_send, b_recv.at[0, 0], dev_z[0]).wait_send()
    pl.when(((z == 4) | (z == 7)))(remote(bbuf.at[0, pl.ds(0, BS)], b_send, b_recv.at[0, 0], dev_z[0]).wait_send)
    pl.when(((z == 0) | (z == 3) | (z == 5) | (z == 6)))(remote(bbuf.at[pl.ds(0, 1)], b_send, b_recv.at[0, 0], dev_z[0]).wait_send)
    pl.when(((z == 1) | (z == 2)))(remote(abuf.at[0, pl.ds(0, BS)], b_send, b_recv.at[0, 0], dev_z[0]).wait_send)
    pl.when(((z == 1) | (z == 2)))(remote(bbuf.at[pl.ds(0, 1)], b_send, b_recv.at[0, 0], dev_z[0]).wait_send)
    remote(abuf.at[pl.ds(0, 30)], a_send, a_recv.at[0], dev_d).wait_send()


def solution(mesh):
    nz = mesh.shape["row"]
    nx = mesh.shape["col"] // 4

    def per_device(a, am, b, bm):
        rows = am.shape[0]
        ncol = nx * 4
        depth = b.shape[0]
        width = b.shape[1] // 2
        am = am.reshape(1, rows)
        return pl.pallas_call(
            functools.partial(kernel, nz, nx, rows),
            out_shape=jax.ShapeDtypeStruct((a.shape[0], width), jnp.bfloat16),
            in_specs=[pl.BlockSpec(memory_space=pl.ANY)] * 4,
            out_specs=pl.BlockSpec(memory_space=pltpu.VMEM),
            scratch_shapes=[
                pltpu.VMEM(a.shape, jnp.bfloat16),
                pltpu.VMEM((depth, width), jnp.bfloat16),
                pltpu.SMEM(am.shape, jnp.int32),
                pltpu.SMEM(bm.shape, jnp.int32),
                pltpu.VMEM((2 * ncol, BS + CODE, BS), jnp.bfloat16),
                pltpu.VMEM((nz, depth, width), jnp.bfloat16),
                pltpu.VMEM((nz, a.shape[0], 2 * BS), jnp.bfloat16),
                pltpu.VMEM((a.shape[0], width), jnp.float32),
                pltpu.SemaphoreType.DMA((4,)),
                pltpu.SemaphoreType.DMA,
                pltpu.SemaphoreType.DMA((D_FIRST + 8,)),
                pltpu.SemaphoreType.DMA,
                pltpu.SemaphoreType.DMA((2, (nz // 2 - 1) * len(CHUNKS) + 1)),
            ],
            compiler_params=pltpu.CompilerParams(
                collective_id=0, has_side_effects=True, vmem_limit_bytes=46 * 2**20
            ),
        )(*(pltpu.with_memory_space_constraint(v, pltpu.HBM) for v in (a, am, b, bm)))

    spec = P("row", "col")
    return jax.shard_map(
        per_device,
        mesh=mesh,
        in_specs=(spec, spec, spec, spec),
        out_specs=P("row", ("col", "rep")),
        check_vma=False,
    )
```

```python
import functools

import jax
import jax.numpy as jnp
from jax import lax
from jax.experimental import pallas as pl
from jax.experimental.pallas import tpu as pltpu
from jax.sharding import PartitionSpec as P

BS = 256
HALF = BS // 2
TILE = 64
CODE = 16
CHUNKS = ((0, 128), (256, 128), (384, 128), (128, 128))
WAYS = (0, 1, 1, 0)
X_FIRST, X_FAR, Y_OWN, Y_FIRST, Y_FAR, D_FIRST = 0, 4, 6, 8, 12, 14
MESH = pl.DeviceIdType.MESH


def kernel(
    nz, nx, rows,
    a_ref, am_ref, b_ref, bm_ref, c_ref,
    avm, bvm, ams, bms, abuf, bbuf, dense, acc,
    load_sem, a_send, a_recv, b_send, b_recv,
):
    z = lax.axis_index("row")
    col = lax.axis_index("col")
    rep = lax.axis_index("rep")
    x = col // 4
    yl = (col // 2) % 2
    core = col % 2
    width = BS
    far = nz // 2

    def col_of(xx, yy, cc):
        return xx * 4 + yy * 2 + cc

    xs = [x, (x + nx - 1) % nx, (x + 1) % nx, (x + 2) % nx]
    dev_z = ({"row": (z + 1) % nz}, {"row": (z + nz - 1) % nz})
    dev_x = ({"col": col_of(xs[2], yl, core)}, {"col": col_of(xs[1], yl, core)})
    dev_y = (
        {"col": col_of(x, 1 - yl, core), "rep": rep},
        {"col": col_of(x, 1 - yl, core), "rep": 1 - rep},
    )
    dev_d = {"col": col_of(x, yl, 1 - core)}
    peers = [*dev_z, *dev_x, *dev_y, dev_d]

    load_bm = pltpu.make_async_copy(bm_ref, bms, load_sem.at[0])
    load_am = pltpu.make_async_copy(am_ref, ams, load_sem.at[1])
    load_b = pltpu.make_async_copy(
        b_ref.at[:, pl.ds(pl.multiple_of(rep * width, width), width)], bvm, load_sem.at[2]
    )
    load_a = pltpu.make_async_copy(a_ref, avm, load_sem.at[3])
    for copy in (load_bm, load_b, load_am, load_a):
        copy.start()

    barrier = pltpu.get_barrier_semaphore()
    for peer in peers:
        pl.semaphore_signal(barrier, inc=1, device_id=peer, device_id_type=MESH)

    def remote(piece, send_sem, recv_sem, dev):
        return pltpu.make_async_remote_copy(
            src_ref=piece,
            dst_ref=piece,
            send_sem=send_sem,
            recv_sem=recv_sem,
            device_id=dev,
            device_id_type=MESH,
        )

    first = jnp.where((z + nz // 4) % nz < nz // 2, 1, 0)
    second = 1 - first

    def b_send_to(source, j, way, hop):
        sem = b_recv.at[way, (hop - 1) * len(CHUNKS) + j] if hop < far else b_recv.at[0, (far - 1) * len(CHUNKS)]
        dev = {"row": (z + nz + 1 - 2 * way) % nz}
        remote(bbuf.at[source, pl.ds(*CHUNKS[j])], b_send, sem, dev).start()

    def b_wait(sem, lines):
        remote(bbuf.at[z, pl.ds(0, lines)], b_send, sem, dev_z[0]).wait_recv()

    def b_half(way, hop, j):
        b_wait(b_recv.at[way, (hop - 1) * len(CHUNKS) + j], CHUNKS[j][1])
        onward = functools.partial(b_send_to, (z + nz + (2 * way - 1) * hop) % nz, j, way, hop + 1)
        if hop + 1 < far:
            onward()
        else:
            to = (z + nz + 1 - 2 * way) % nz
            takes = WAYS[j]
            takes = jnp.where(((to == 0)), 1, takes)
            takes = jnp.where(((to == 3)), 0, takes)
            pl.when(way == takes)(onward)

    def b_step(hop, j):
        b_half(first, hop, j)
        b_half(second, hop, j)

    def a_send_to(item, slot, part, sem, dev):
        start, size = ((0, BS + CODE), (0, HALF), (HALF, HALF + CODE))[part]
        remote(abuf.at[2 * item + slot, pl.ds(start, size)], a_send, a_recv.at[sem], dev).start()

    def y_send(item, slot, part, sem):
        a_send_to(item, slot, part, sem, dev_y[(slot + part) % 2])

    def d_send(n, item, slot):
        a_send_to(item, slot, 0, D_FIRST + n, dev_d)

    def x_send(item, slot, part, way, sem):
        a_send_to(item, slot, part, sem, dev_x[way])

    def a_wait(sem, part):
        b_wait(a_recv.at[sem], 2 * (0, HALF, HALF + CODE)[part])

    acc[...] = jnp.zeros_like(acc)
    load_bm.wait()
    load_b.wait()
    for start, size in CHUNKS:
        keep = jnp.full((size, width), bms[start // BS, rep].astype(jnp.float32))
        bbuf[z, pl.ds(start, size), :] = bvm[pl.ds(start, size), :] * keep.astype(jnp.bfloat16)
    pl.semaphore_wait(barrier, len(peers))
    for j in range(len(CHUNKS)):
        for way in range(2):
            b_send_to(z, j, way, 1)

    load_am.wait()
    count = jnp.int32(0)
    lines = lax.broadcasted_iota(jnp.int32, (CODE, BS), 0)
    code = [jnp.zeros((CODE, BS), jnp.float32)] * 2
    weights = []
    for i in range(rows):
        m = ams[0, i]
        later = jnp.minimum(count, 1)
        count = count + m
        pair = [jnp.full((CODE, BS), (m * w).astype(jnp.float32)) for w in (1 - later, later)]
        code = [c + jnp.where(lines == i, p, 0.0) for c, p in zip(code, pair)]
        weights.append([p.astype(jnp.bfloat16) for p in pair])
    load_a.wait()

    def pack(t, _):
        at = pl.multiple_of(t * 4 * CODE, 4 * CODE)
        total = [None, None]
        for i in range(rows):
            part = avm[pl.ds(at + i * BS, 4 * CODE), :].reshape(4, CODE, BS)
            for slot in range(2):
                term = part * weights[i][slot][None]
                total[slot] = term if i == 0 else total[slot] + term
        for slot in range(2):
            abuf[2 * col + slot, pl.ds(at, 4 * CODE), :] = total[slot].reshape(4 * CODE, BS)
        return 0

    lax.fori_loop(0, BS // (4 * CODE), pack, 0)
    for slot in range(2):
        abuf[2 * col + slot, pl.ds(BS, CODE), :] = code[slot].astype(jnp.bfloat16)
    for turn in range(4):
        for way in range(2):
            x_send(col, (turn // 2 + way) % 2, turn % 2 + 1, way, X_FIRST + turn)
        if turn < 2:
            for slot in range(2):
                y_send(col, slot, turn + 1, Y_OWN + turn)
    for slot in range(2):
        d_send(0, col, slot)

    mine = [col_of(xx, yl, core) for xx in xs]
    other = [col_of(xx, 1 - yl, core) for xx in xs]

    def x_arrival(turn):
        part = turn % 2 + 1
        a_wait(X_FIRST + turn, part)
        for n in (1, 2):
            slot = (turn // 2 + n - 1) % 2
            y_send(mine[n], slot, part, Y_FIRST + turn)
            if turn < 2:
                x_send(mine[n], slot, part, n - 1, X_FAR + turn)
            if part == 2:
                d_send(n, mine[n], slot)

    def x_second(part):
        a_wait(X_FAR + part - 1, part)
        for slot in range(2):
            if part == 1:
                y_send(mine[3], slot, part, Y_FAR)
            else:
                d_send(3, mine[3], slot)

    def y_own():
        for part in (1, 2):
            a_wait(Y_OWN + part - 1, part)
        for slot in range(2):
            d_send(4, other[0], slot)

    def y_arrival(turn):
        part = turn % 2 + 1
        a_wait(Y_FIRST + turn, part)
        if part == 2:
            for n in (1, 2):
                slot = (turn // 2 + n - 1) % 2
                if slot == n - 1:
                    x_send(other[n], slot, part, n - 1, Y_FAR + 1)
                d_send(4 + n, other[n], slot)

    def y_far():
        for part in (2, 1):
            a_wait(Y_FAR + part - 1, part)
        for slot in range(2):
            d_send(7, other[3], slot)

    def expand(n, far_y):
        xx = xs[n]
        yy = 1 - yl if far_y else yl
        remote(abuf.at[pl.ds(0, 2)], a_send, a_recv.at[D_FIRST + n + 4 * far_y], dev_d).wait_recv()

        weights = []
        for cc in range(2):
            for slot in range(2):
                line = abuf[2 * col_of(xx, yy, cc) + slot, pl.ds(BS, CODE), :].astype(jnp.float32)
                weights.append(
                    [jnp.broadcast_to(line[r : r + 1], (CODE, BS)).astype(jnp.bfloat16)[None] for r in range(rows)]
                )

        def body(t, _):
            at = pl.multiple_of(t * TILE, TILE)
            for cc in range(2):
                k = col_of(xx, yy, cc)
                one, two = (
                    abuf[2 * k + slot, pl.ds(at, TILE), :].reshape(TILE // CODE, CODE, BS) for slot in range(2)
                )
                for r in range(rows):
                    total = one * weights[2 * cc][r] + two * weights[2 * cc + 1][r]
                    dense[xx * 2 + yy, pl.ds(at + r * BS, TILE), pl.ds(cc * BS, BS)] = total.reshape(TILE, BS)
            return 0

        lax.fori_loop(0, BS // TILE, body, 0)

    def multiply(panels, hops, panels_before=0, hops_before=0):
        def body(i, _):
            source = (z + nz + i - hops) % nz
            n = (source // 2 + nx - x) % nx
            near = jnp.where(source % 2 == yl, 1, 0)
            place = jnp.where(n == 0, 1 - near, jnp.where(n == nx - 1, 0, n) + 5 - 3 * near)
            far_off = jnp.abs(i - hops)
            ready = place < panels
            done = (far_off <= hops_before) & (place < panels_before)

            @pl.when(ready & jnp.logical_not(done))
            def _():
                acc[...] += jnp.dot(dense[source], bbuf[source], preferred_element_type=jnp.float32)

            return 0

        lax.fori_loop(0, 2 * hops + 1, body, 0)

    expand(0, 0)
    b_half(first, 1, 0)
    b_half(first, 1, 1)
    b_half(second, 1, 0)
    x_arrival(0)
    b_half(first, 1, 2)
    b_half(second, 1, 1)
    x_arrival(1)
    y_own()
    b_half(first, 1, 3)
    b_half(second, 1, 2)
    x_arrival(2)
    expand(0, 1)
    b_half(first, 2, 0)
    b_half(second, 1, 3)
    y_arrival(0)
    x_arrival(3)
    multiply(2, 1, 0, 0)
    b_half(first, 2, 1)
    b_half(second, 2, 0)
    y_arrival(1)
    x_second(1)
    expand(1, 0)
    b_half(first, 2, 2)
    b_half(second, 2, 1)
    y_arrival(2)
    x_second(2)
    expand(2, 0)
    multiply(4, 1, 2, 1)
    b_half(first, 2, 3)
    b_half(second, 2, 2)
    y_arrival(3)
    expand(3, 0)
    b_half(first, 3, 0)
    b_half(second, 2, 3)
    expand(1, 1)
    multiply(6, 2, 4, 1)
    y_far()
    b_half(first, 3, 1)
    b_half(second, 3, 0)
    expand(2, 1)
    multiply(7, 2, 6, 2)
    expand(3, 1)
    b_half(first, 3, 2)
    b_half(second, 3, 1)
    b_half(first, 3, 3)
    b_half(second, 3, 2)
    multiply(8, 2, 7, 2)
    b_half(second, 3, 3)
    multiply(8, 3, 8, 2)
    b_wait(b_recv.at[0, (far - 1) * len(CHUNKS)], b_ref.shape[0])
    last = (z + far) % nz
    total = jnp.dot(dense[last], bbuf[last], preferred_element_type=jnp.float32)
    c_ref[...] = (acc[...] + total).astype(jnp.bfloat16)
    remote(bbuf.at[pl.ds(0, nz - 2)], b_send, b_recv.at[0, 0], dev_z[0]).wait_send()
    pl.when(((z == 4) | (z == 7)))(remote(bbuf.at[0, pl.ds(0, BS)], b_send, b_recv.at[0, 0], dev_z[0]).wait_send)
    pl.when(((z == 0) | (z == 3) | (z == 5) | (z == 6)))(remote(bbuf.at[pl.ds(0, 1)], b_send, b_recv.at[0, 0], dev_z[0]).wait_send)
    pl.when(((z == 1) | (z == 2)))(remote(abuf.at[0, pl.ds(0, BS)], b_send, b_recv.at[0, 0], dev_z[0]).wait_send)
    pl.when(((z == 1) | (z == 2)))(remote(bbuf.at[pl.ds(0, 1)], b_send, b_recv.at[0, 0], dev_z[0]).wait_send)
    remote(abuf.at[pl.ds(0, 30)], a_send, a_recv.at[0], dev_d).wait_send()


def solution(mesh):
    nz = mesh.shape["row"]
    nx = mesh.shape["col"] // 4

    def per_device(a, am, b, bm):
        rows = am.shape[0]
        ncol = nx * 4
        depth = b.shape[0]
        width = b.shape[1] // 2
        am = am.reshape(1, rows)
        return pl.pallas_call(
            functools.partial(kernel, nz, nx, rows),
            out_shape=jax.ShapeDtypeStruct((a.shape[0], width), jnp.bfloat16),
            in_specs=[pl.BlockSpec(memory_space=pl.ANY)] * 4,
            out_specs=pl.BlockSpec(memory_space=pltpu.VMEM),
            scratch_shapes=[
                pltpu.VMEM(a.shape, jnp.bfloat16),
                pltpu.VMEM((depth, width), jnp.bfloat16),
                pltpu.SMEM(am.shape, jnp.int32),
                pltpu.SMEM(bm.shape, jnp.int32),
                pltpu.VMEM((2 * ncol, BS + CODE, BS), jnp.bfloat16),
                pltpu.VMEM((nz, depth, width), jnp.bfloat16),
                pltpu.VMEM((nz, a.shape[0], 2 * BS), jnp.bfloat16),
                pltpu.VMEM((a.shape[0], width), jnp.float32),
                pltpu.SemaphoreType.DMA((4,)),
                pltpu.SemaphoreType.DMA,
                pltpu.SemaphoreType.DMA((D_FIRST + 8,)),
                pltpu.SemaphoreType.DMA,
                pltpu.SemaphoreType.DMA((2, (nz // 2 - 1) * len(CHUNKS) + 1)),
            ],
            compiler_params=pltpu.CompilerParams(
                collective_id=0, has_side_effects=True, vmem_limit_bytes=46 * 2**20
            ),
        )(*(pltpu.with_memory_space_constraint(v, pltpu.HBM) for v in (a, am, b, bm)))

    spec = P("row", "col")
    return jax.shard_map(
        per_device,
        mesh=mesh,
        in_specs=(spec, spec, spec, spec),
        out_specs=P("row", ("col", "rep")),
        check_vma=False,
    )
```
